32 devices in a mesh: groups: 2 (over x), wide: 8 (over z, y), narrow: 2 (over core).
Axes of the slice: x: 2, y: 2, z: 4, core: 2. Of those that a mesh axis runs over, the one named last changes fastest.
Arguments:
- tokens: bfloat16 [1024, 18432], P(('groups', 'narrow'), 'wide'), parts along dimension 0, may hold values from -6 to 6
- w_query: bfloat16 [18432, 7168], P('wide', 'narrow'), may hold values from -0.046875 to 0.046875
- w_keyval: bfloat16 [18432, 512], P('wide'), may hold values from -0.09375 to 0.09375
- cache_keys: bfloat16 [1024, 256, 256], P(('groups', 'wide')), parts along dimension 0, may hold values from -300 to 300
- cache_values: bfloat16 [1024, 256, 256], P(('groups', 'wide')), parts along dimension 0, may hold values from -24 to 24
- w_out: bfloat16 [7168, 18432], P('narrow', 'wide'), may hold values from -0.0625 to 0.0625
Outputs:
- attended: bfloat16 [1024, 18432], P(('groups', 'narrow'), 'wide'), parts along dimension 0
The draws below stay inside these ranges and needn't reach their ends.
There are 2 independent parts, one for each index of `groups`. The reference program is written for one: setup_inputs(seed, part) draws one part's arguments, and reference() takes and returns one part's arrays. A program takes and returns all parts, laid end to end along the dimension named above; an argument that names none is the same for every part. Nothing has to cross between parts.
All inputs are finite; a program needn't handle non-finite values.
Results may differ from the reference program's by a relative error of at most 0.012.
The reference program's roundings to bfloat16 on the way count: a program that leaves them out, or rounds other values in their place, can miss the bound.
Values may be sent and summed in bfloat16 or wider, within the bound.
A program may use at most 192 MiB of HBM per device.

```python
import jax
import jax.numpy as jnp

D = 18432
DH = 256
HEADS = 28
ROWS = 512
LEN = 256
QH = 7168


def draw_cache_keys(key, part):
    key = jax.random.fold_in(key, 7)
    base = jax.random.normal(key, (ROWS, LEN, DH), jnp.float32)
    base = jnp.clip(base, -300.0, 300.0)
    return base.astype(jnp.bfloat16)


def level_of(stream_key, extent, shards, least, largest):
    gain, own = 1.0, jax.random.fold_in(stream_key, 6)
    for dim, shards_of in shards:
        draws = jnp.exp(jax.random.uniform(jax.random.fold_in(own, dim), (shards_of,), jnp.float32, least / len(shards), largest / len(shards)))
        gain = gain * jnp.repeat(draws, extent[dim] // shards_of).reshape([-1 if axis == dim else 1 for axis in range(len(extent))])
    return gain


def scatter_about(key, dims, width, most, split=(), held_as=jnp.bfloat16):
    loudness = level_of(key, dims, split, -0.22, 0.18) if split else 1.0
    drawn = jax.random.normal(key, dims, jnp.float32) * width * loudness
    return jnp.minimum(jnp.maximum(drawn, -most), most).astype(held_as)


def setup_inputs(seed: int = 0, part: int = 0) -> dict:
    arg_keys = jax.random.split(jax.random.key(seed), 7)
    own_keys = jax.random.split(jax.random.fold_in(arg_keys[6], part), 7)
    tokens = scatter_about(own_keys[0], (ROWS, D), 1.0, 6.0, ((0, 2), (1, 8)))
    w_query = scatter_about(arg_keys[1], (D, QH), D ** -0.5, 0.046875, ((0, 8), (1, 2)))
    w_keyval = scatter_about(arg_keys[2], (D, 2 * DH), (D // 4) ** -0.5, 0.09375, ((0, 8),))
    cache_keys = draw_cache_keys(jax.random.fold_in(jax.random.fold_in(arg_keys[6], part), 71), part)
    cache_values = scatter_about(own_keys[4], (ROWS, LEN, DH), 4.0, 24.0, ((0, 8),))
    w_out = scatter_about(arg_keys[5], (QH, D), QH ** -0.5, 0.0625, ((0, 2), (1, 8)))
    return dict(tokens=tokens, w_query=w_query, w_keyval=w_keyval, cache_keys=cache_keys, cache_values=cache_values, w_out=w_out)


def reference(tokens, w_query, w_keyval, cache_keys, cache_values, w_out):
    query = jnp.dot(tokens, w_query, preferred_element_type=jnp.float32).astype(jnp.bfloat16)
    keyval = jnp.dot(tokens, w_keyval, preferred_element_type=jnp.float32).astype(jnp.bfloat16)
    new_key = keyval[:, :DH].astype(jnp.float32)
    new_value = keyval[:, DH:].astype(jnp.float32)
    heads_q = query.reshape(ROWS, HEADS, DH).astype(jnp.float32)
    scale = DH ** -0.5
    cached = jnp.einsum("rhd,rld->rhl", heads_q, cache_keys.astype(jnp.float32)) * scale
    own = jnp.einsum("rhd,rd->rh", heads_q, new_key) * scale
    top = jnp.maximum(jnp.max(cached, axis=-1), own)
    cached_exp = jnp.exp(cached - top[:, :, None])
    own_exp = jnp.exp(own - top)
    total = jnp.sum(cached_exp, axis=-1) + own_exp
    probs_cached = (cached_exp / total[:, :, None]).astype(jnp.bfloat16).astype(jnp.float32)
    probs_own = (own_exp / total).astype(jnp.bfloat16).astype(jnp.float32)
    mixed = jnp.einsum("rhl,rld->rhd", probs_cached, cache_values.astype(jnp.float32))
    mixed = mixed + probs_own[:, :, None] * new_value[:, None, :]
    mixed = mixed.astype(jnp.bfloat16).reshape(ROWS, QH)
    return jnp.dot(mixed, w_out, preferred_element_type=jnp.float32).astype(jnp.bfloat16)
```

```python
import functools
import math

import jax
import jax.numpy as jnp
from jax import lax
from jax.experimental import pallas as pl
from jax.experimental.pallas import tpu as pltpu
from jax.sharding import PartitionSpec as P

MESH = pl.DeviceIdType.MESH
F32 = jnp.float32
BF16 = jnp.bfloat16
LAG = 3
BLOCK = 128


def bound_shift(width):
    return 15 - math.ceil(math.log2(2 * width * 6.0 * 0.09375))


def encode(x, shift):
    x = x * 2.0**shift
    x2 = x * x
    x4 = x2 * x2
    x8 = x4 * x4
    return jnp.where(x < 0, -x8, x8).astype(BF16)


def decode(y, shift):
    y = y.astype(F32)
    x = jnp.exp2(jnp.log2(jnp.abs(y)) * 0.125 - shift)
    return jnp.where(y < 0, -x, x)


def wait_bytes(ref, sem):
    pltpu.make_async_copy(ref, ref, sem).wait()


def peers(wide):
    outers = wide // 2
    me = lax.axis_index("wide")
    outer, inner = me // 2, me % 2
    partner = outer * 2 + 1 - inner
    others = [lax.rem(outer + k, outers) for k in range(1, outers)]
    return outers, me, outer, inner, partner, others


def greet(wide):
    outers, _, _, inner, partner, others = peers(wide)
    barrier = pltpu.get_barrier_semaphore()
    pl.semaphore_signal(barrier, inc=1, device_id={"narrow": 1 - lax.axis_index("narrow")}, device_id_type=MESH)
    pl.semaphore_signal(barrier, inc=1, device_id={"wide": partner}, device_id_type=MESH)
    for other in others:
        pl.semaphore_signal(barrier, inc=1, device_id={"wide": other * 2 + inner}, device_id_type=MESH)
    pl.semaphore_wait(barrier, 1 + outers)


def remote(src, dst, send, recv, where):
    return pltpu.make_async_remote_copy(
        src_ref=src, dst_ref=dst, send_sem=send, recv_sem=recv, device_id=where, device_id_type=MESH
    )


def project_kernel(
    wide, dh, tokens, w_query, w_keyval, query, keyval,
    tok, weights, product, mine, kept, pair_out, pair_in, line_out, line_in, new,
    w_sem, tok_sem, pair_send, pair_recv, line_send, line_recv, new_sem,
):
    outers, _, outer, inner, partner, others = peers(wide)
    half = lax.axis_index("narrow")
    chunks, rows = pair_out.shape[0], kept.shape[1]
    heads = chunks - 1
    width = tokens.shape[1]
    shift = bound_shift(width)

    def head_copy(h):
        columns = pl.ds(pl.multiple_of(h * dh, dh), dh)
        return pltpu.make_async_copy(w_query.at[:, columns], weights.at[h + 1], w_sem.at[h + 1])

    own_tokens = pltpu.make_async_copy(tokens, tok.at[half], tok_sem.at[0])
    own_tokens.start()
    columns = pl.ds(pl.multiple_of(half * dh, dh), dh)
    pltpu.make_async_copy(w_keyval.at[:, columns], weights.at[0], w_sem.at[0]).start()
    greet(wide)
    across = {"narrow": 1 - half}
    pair_tokens = remote(tokens, tok.at[half], tok_sem.at[1], tok_sem.at[2], across)
    pair_tokens.start()

    @pl.loop(0, heads)
    def _(h):
        head_copy(h).start()

    own_tokens.wait()
    pair_tokens.wait_recv()

    def pair_copy(c):
        return remote(pair_out.at[c], pair_in.at[c], pair_send, pair_recv.at[c], {"wide": partner})

    @pl.loop(0, chunks + 2 * LAG)
    def _(t):
        @pl.when(t < chunks)
        def _():
            wait_bytes(weights.at[t], w_sem.at[t])
            product[...] = jnp.dot(
                tok[...].reshape(wide * rows, width), weights[t], preferred_element_type=F32
            ).reshape(wide, rows, dh)
            for o in range(outers):
                pair_out[t, o] = encode(product[2 * o + 1 - inner], shift)
                mine[t, o] = product[2 * o + inner]
            pair_copy(t).start()

        @pl.when(jnp.logical_and(t >= LAG, t < chunks + LAG))
        def _():
            c = t - LAG
            wait_bytes(pair_in.at[c], pair_recv.at[c])
            for k, other in enumerate(others):
                line_out[c, k] = encode(mine[c, other] + decode(pair_in[c, other], shift), shift)
                remote(
                    line_out.at[c, k], line_in.at[c, k], line_send, line_recv.at[c], {"wide": other * 2 + inner}
                ).start()
            kept[c] = mine[c, outer] + decode(pair_in[c, outer], shift)

        @pl.when(t >= 2 * LAG)
        def _():
            c = t - 2 * LAG
            wait_bytes(line_in.at[c], line_recv.at[c])
            total = kept[c]
            for k in range(outers - 1):
                total += decode(line_in[c, k], shift)
            total = total.astype(BF16)

            @pl.when(c == 0)
            def _():
                new[half] = total
                remote(new.at[half], new.at[half], new_sem.at[0], new_sem.at[1], across).start()

            @pl.when(c > 0)
            def _():
                query[:, pl.ds(pl.multiple_of((c - 1) * dh, dh), dh)] = total

    pair_tokens.wait_send()
    new_copy = remote(new.at[half], new.at[half], new_sem.at[0], new_sem.at[1], across)
    new_copy.wait_recv()
    keyval[:, :dh] = new[0]
    keyval[:, dh:] = new[1]
    new_copy.wait_send()
    wait_bytes(pair_out, pair_send)
    wait_bytes(line_out, line_send)


def project(wide, dh, tokens, w_query, w_keyval):
    width = tokens.shape[1]
    total_rows = 2 * tokens.shape[0]
    rows = total_rows // wide
    outers = wide // 2
    heads = w_query.shape[1] // dh
    chunks = heads + 1
    dma = pltpu.SemaphoreType.DMA
    return pl.pallas_call(
        functools.partial(project_kernel, wide, dh),
        out_shape=[
            jax.ShapeDtypeStruct((rows, heads * dh), BF16),
            jax.ShapeDtypeStruct((rows, 2 * dh), BF16),
        ],
        in_specs=[pl.BlockSpec(memory_space=pl.ANY)] * 3,
        out_specs=[pl.BlockSpec(memory_space=pltpu.VMEM)] * 2,
        scratch_shapes=[
            pltpu.VMEM((2, total_rows // 2, width), BF16),
            pltpu.VMEM((chunks, width, dh), BF16),
            pltpu.VMEM((wide, rows, dh), F32),
            pltpu.VMEM((chunks, outers, rows, dh), F32),
            pltpu.VMEM((chunks, rows, dh), F32),
            pltpu.VMEM((chunks, outers, rows, dh), BF16),
            pltpu.VMEM((chunks, outers, rows, dh), BF16),
            pltpu.VMEM((chunks, outers - 1, rows, dh), BF16),
            pltpu.VMEM((chunks, outers - 1, rows, dh), BF16),
            pltpu.VMEM((2, rows, dh), BF16),
            dma((chunks,)),
            dma((3,)),
            dma,
            dma((chunks,)),
            dma,
            dma((chunks,)),
            dma((2,)),
        ],
        compiler_params=pltpu.CompilerParams(
            collective_id=0, has_side_effects=True, vmem_limit_bytes=60 * 2**20
        ),
        cost_estimate=pl.CostEstimate(
            flops=2 * total_rows * width * chunks * dh, bytes_accessed=2 * width * chunks * dh, transcendentals=0
        ),
    )(tokens, w_query, w_keyval)


def output_kernel(
    wide, mixed, w_out, result,
    gathered, weights, total, half_out, half_in,
    w_sem, send, line_recv, pair_recv, half_send, half_recv,
):
    outers, me, _, inner, partner, others = peers(wide)
    half = lax.axis_index("narrow")
    chunks, _, rows, cols = gathered.shape
    blocks = half_out.shape[0]

    @pl.loop(0, chunks)
    def _(g):
        pltpu.make_async_copy(
            w_out.at[pl.ds(pl.multiple_of(g * cols, cols), cols), :], weights.at[g], w_sem.at[g]
        ).start()
        gathered[g, me] = mixed[:, pl.ds(pl.multiple_of(g * cols, cols), cols)]

    greet(wide)

    def spread(g, block, where, recv):
        remote(gathered.at[g, block], gathered.at[g, block], send, recv, {"wide": where}).start()

    @pl.loop(0, chunks)
    def _(g):
        for other in others:
            spread(g, me, other * 2 + inner, line_recv.at[g])
        spread(g, me, partner, pair_recv.at[g])

    total[...] = jnp.zeros_like(total)

    def product(g, b):
        per = BLOCK // rows
        left = gathered[g, pl.ds(b * per, per)].reshape(BLOCK, cols)
        return jnp.dot(left, weights[g], preferred_element_type=F32)

    def arrive(g):
        wait_bytes(gathered.at[g, pl.ds(0, outers)], pair_recv.at[g])
        wait_bytes(weights.at[g], w_sem.at[g])

    @pl.loop(0, chunks)
    def _(g):
        wait_bytes(gathered.at[g, pl.ds(0, outers - 1)], line_recv.at[g])
        for other in others:
            spread(g, other * 2 + inner, partner, pair_recv.at[g])

        @pl.when(g > 0)
        def _():
            arrive(g - 1)

            @pl.loop(0, 2 * blocks)
            def _(b):
                total[b] += product(g - 1, b)

    last = chunks - 1
    arrive(last)

    def half_copy(b):
        return remote(half_out.at[b], half_in.at[b], half_send, half_recv.at[b], {"narrow": 1 - half})

    @pl.loop(0, blocks)
    def _(b):
        at = (1 - half) * blocks + b
        half_out[b] = (total[at] + product(last, at)).astype(BF16)
        half_copy(b).start()

    @pl.loop(0, blocks)
    def _(b):
        at = half * blocks + b
        own = total[at] + product(last, at)
        wait_bytes(half_in.at[b], half_recv.at[b])
        result[b] = (own + half_in[b].astype(F32)).astype(BF16)

    wait_bytes(half_out, half_send)
    wait_bytes(gathered.at[:, pl.ds(0, 2 * outers - 1)], send)


def project_out(wide, mixed, w_out):
    rows, features = mixed.shape
    width = w_out.shape[1]
    cols = 512
    chunks = features // cols
    blocks = wide * rows // 2 // BLOCK
    dma = pltpu.SemaphoreType.DMA
    result = pl.pallas_call(
        functools.partial(output_kernel, wide),
        out_shape=jax.ShapeDtypeStruct((blocks, BLOCK, width), BF16),
        in_specs=[pl.BlockSpec(memory_space=pltpu.VMEM), pl.BlockSpec(memory_space=pl.ANY)],
        out_specs=pl.BlockSpec(memory_space=pltpu.VMEM),
        scratch_shapes=[
            pltpu.VMEM((chunks, wide, rows, cols), BF16),
            pltpu.VMEM((chunks, cols, width), BF16),
            pltpu.VMEM((2 * blocks, BLOCK, width), F32),
            pltpu.VMEM((blocks, BLOCK, width), BF16),
            pltpu.VMEM((blocks, BLOCK, width), BF16),
            dma((chunks,)),
            dma,
            dma((chunks,)),
            dma((chunks,)),
            dma,
            dma((blocks,)),
        ],
        compiler_params=pltpu.CompilerParams(
            collective_id=1, has_side_effects=True, vmem_limit_bytes=60 * 2**20
        ),
        cost_estimate=pl.CostEstimate(
            flops=2 * wide * rows * features * width, bytes_accessed=2 * features * width, transcendentals=0
        ),
    )(mixed, w_out)
    return result.reshape(blocks * BLOCK, width)


def attend(query, keyval, cache_keys, cache_values):
    head_size = cache_keys.shape[-1]
    local_rows = query.shape[0]
    local_heads = query.shape[1] // head_size
    heads_q = query.reshape(local_rows, local_heads, head_size)
    new_key = keyval[:, :head_size]
    new_value = keyval[:, head_size:]
    scale = head_size ** (-0.5)
    cached = (
        jnp.einsum("rhd,rld->rhl", heads_q, cache_keys, preferred_element_type=jnp.float32) * scale
    )
    own = jnp.einsum("rhd,rd->rh", heads_q, new_key, preferred_element_type=jnp.float32) * scale
    top = jnp.maximum(jnp.max(cached, axis=-1), own)
    cached_exp = jnp.exp(cached - top[:, :, None])
    own_exp = jnp.exp(own - top)
    total = jnp.sum(cached_exp, axis=-1) + own_exp
    probs_cached = (cached_exp / total[:, :, None]).astype(jnp.bfloat16)
    probs_own = (own_exp / total).astype(jnp.bfloat16)
    mixed = jnp.einsum(
        "rhl,rld->rhd", probs_cached, cache_values, preferred_element_type=jnp.float32
    )
    mixed = (
        mixed
        + probs_own.astype(jnp.float32)[:, :, None] * new_value.astype(jnp.float32)[:, None, :]
    )
    return mixed.astype(jnp.bfloat16).reshape(local_rows, local_heads * head_size)


def shards(wide, tokens, w_query, w_keyval, cache_keys, cache_values, w_out):
    query, keyval = project(wide, cache_keys.shape[-1], tokens, w_query, w_keyval)
    mixed = attend(query, keyval, cache_keys, cache_values)
    return project_out(wide, mixed, w_out)


def solution(mesh):
    in_specs = (
        P(("groups", "narrow"), "wide"),
        P("wide", "narrow"),
        P("wide", None),
        P(("groups", "wide"), None, None),
        P(("groups", "wide"), None, None),
        P("narrow", "wide"),
    )
    out_specs = P(("groups", "narrow"), "wide")
    return jax.shard_map(
        functools.partial(shards, mesh.shape["wide"]),
        mesh=mesh, in_specs=in_specs, out_specs=out_specs, check_vma=False,
    )
```

```python
import functools
import math

import jax
import jax.numpy as jnp
from jax import lax
from jax.experimental import pallas as pl
from jax.experimental.pallas import tpu as pltpu
from jax.sharding import PartitionSpec as P

MESH = pl.DeviceIdType.MESH
F32 = jnp.float32
BF16 = jnp.bfloat16
LAG = 3
SLOTS = LAG + 1
BLOCK = 128
GROUP = 8
BATCH = 8
AHEAD = 3


def bound_shift(width):
    return 15 - math.ceil(math.log2(2 * width * 6.0 * 0.09375))


def encode(x, shift, squarings):
    power = x * 2.0**shift
    for _ in range(squarings):
        power = power * power
    return jnp.where(x < 0, -power, power).astype(BF16)


def decode(y, shift, squarings):
    y = y.astype(F32)
    x = jnp.exp2(jnp.log2(jnp.abs(y)) * 0.5**squarings - shift)
    return jnp.where(y < 0, -x, x)


def wait_bytes(ref, sem):
    pltpu.make_async_copy(ref, ref, sem).wait()


def peers(wide):
    outers = wide // 2
    me = lax.axis_index("wide")
    outer, inner = me // 2, me % 2
    partner = outer * 2 + 1 - inner
    others = [lax.rem(outer + k, outers) for k in range(1, outers)]
    return outers, me, outer, inner, partner, others


def greet(wide):
    outers, _, _, inner, partner, others = peers(wide)
    barrier = pltpu.get_barrier_semaphore()
    pl.semaphore_signal(barrier, inc=1, device_id={"narrow": 1 - lax.axis_index("narrow")}, device_id_type=MESH)
    pl.semaphore_signal(barrier, inc=1, device_id={"wide": partner}, device_id_type=MESH)
    for other in others:
        pl.semaphore_signal(barrier, inc=1, device_id={"wide": other * 2 + inner}, device_id_type=MESH)
    pl.semaphore_wait(barrier, 1 + outers)


def remote(src, dst, send, recv, where):
    return pltpu.make_async_remote_copy(
        src_ref=src, dst_ref=dst, send_sem=send, recv_sem=recv, device_id=where, device_id_type=MESH
    )


def block_kernel(
    wide, tokens, w_query, w_keyval, cache_keys, cache_values, w_out, result,
    tok, weights, product, mine, kept, pair_out, pair_in, line_out, line_in, new, new_wide,
    query, mixed, keys, values, gathered, out_weights, total, half_out, half_in,
    w_sem, tok_sem, cache_sem, pair_send, pair_recv, line_send, line_recv, new_sem,
    out_sem, spread_send, spread_line, spread_pair, half_send, half_recv,
):
    outers, me, outer, inner, partner, others = peers(wide)
    half = lax.axis_index("narrow")
    across = {"narrow": 1 - half}
    chunks, _, rows, dh = pair_out.shape
    heads = chunks - 1
    width = tokens.shape[1]
    shift = bound_shift(width)
    scale = dh**-0.5
    pieces, cols = gathered.shape[0], gathered.shape[3]
    blocks = half_out.shape[0]
    batches = rows // BATCH
    first_heads = min(GROUP, heads)
    rest_heads = heads - first_heads
    begin = first_heads + 2 * LAG + 1
    per = -(-batches // 3)

    def weight_copy(c, slot):
        columns = pl.ds(pl.multiple_of((c - 1) * dh, dh), dh)
        return pltpu.make_async_copy(w_query.at[:, columns], weights.at[slot], w_sem.at[slot])

    def out_copy(g):
        take = pl.ds(pl.multiple_of(g * cols, cols), cols)
        slot = g % AHEAD
        return pltpu.make_async_copy(w_out.at[take, :], out_weights.at[slot], out_sem.at[slot])

    own_tokens = pltpu.make_async_copy(tokens, tok.at[half], tok_sem.at[0])
    own_tokens.start()
    columns = pl.ds(pl.multiple_of(half * dh, dh), dh)
    pltpu.make_async_copy(w_keyval.at[:, columns], weights.at[0], w_sem.at[0]).start()
    greet(wide)
    pair_tokens = remote(tokens, tok.at[half], tok_sem.at[1], tok_sem.at[2], across)
    pair_tokens.start()

    @pl.loop(1, SLOTS)
    def _(c):
        weight_copy(c, c).start()

    key_copy = pltpu.make_async_copy(cache_keys, keys, cache_sem.at[0])
    value_copy = pltpu.make_async_copy(cache_values, values, cache_sem.at[1])
    query[...] = jnp.zeros_like(query)
    own_tokens.wait()
    pair_tokens.wait_recv()

    new_copy = remote(new.at[half], new.at[half], new_sem.at[0], new_sem.at[1], across)

    def spread(g, block, where, recv):
        remote(
            gathered.at[g, block], gathered.at[g, block], spread_send, recv, {"wide": where}
        ).start()

    def forward(g):
        wait_bytes(gathered.at[g, pl.ds(0, outers - 1)], spread_line.at[g])
        for other in others:
            spread(g, other * 2 + inner, partner, spread_pair.at[g])

    def attend(group, b):
        take = pl.ds(pl.multiple_of(b * BATCH, BATCH), BATCH)
        q = query[group, take]
        cached = lax.dot_general(
            q.astype(BF16), keys[take], (((2,), (2,)), ((0,), (0,))), preferred_element_type=F32
        ) * scale
        new_key = new_wide[0, take][:, None, :]
        new_value = new_wide[1, take][:, None, :]
        own = jnp.sum(q * new_key, axis=-1, keepdims=True) * scale
        top = jnp.maximum(jnp.max(cached, axis=-1, keepdims=True), own)
        cached_exp = jnp.exp(cached - top)
        own_exp = jnp.exp(own - top)
        denominator = jnp.sum(cached_exp, axis=-1, keepdims=True) + own_exp
        probs = (cached_exp / denominator).astype(BF16)
        probs_own = (own_exp / denominator).astype(BF16).astype(F32)
        out = lax.dot_general(
            probs, values[take], (((2,), (1,)), ((0,), (0,))), preferred_element_type=F32
        )
        mixed[take] = out + probs_own * new_value

    def spread_group(first, count):
        for j in range(count):
            piece, at = divmod((first + j) * dh, cols)
            gathered[piece, me, :, at : at + dh] = mixed[:, j, :].astype(BF16)
        for g in range(first * dh // cols, (first + count) * dh // cols):
            for other in others:
                spread(g, me, other * 2 + inner, spread_line.at[g])
            spread(g, me, partner, spread_pair.at[g])

    @pl.loop(0, max(chunks + 2 * LAG, begin + 3))
    def _(t):
        @pl.when(t < chunks)
        def _():
            slot = t % SLOTS
            wait_bytes(weights.at[slot], w_sem.at[slot])
            product[...] = jnp.dot(
                tok[...].reshape(wide * rows, width), weights[slot], preferred_element_type=F32
            ).reshape(wide, rows, dh)
            for o in range(outers):
                pair_out[t, o] = encode(product[2 * o + 1 - inner], shift, 3)
                mine[slot, o] = product[2 * o + inner]
            remote(pair_out.at[t], pair_in.at[t], pair_send, pair_recv.at[t], {"wide": partner}).start()

            @pl.when(t + SLOTS < chunks)
            def _():
                weight_copy(t + SLOTS, slot).start()

        @pl.when(t == LAG)
        def _():
            key_copy.start()
            value_copy.start()

            @pl.loop(0, AHEAD)
            def _(g):
                out_copy(g).start()

        @pl.when(t == begin)
        def _():
            key_copy.wait()
            value_copy.wait()
            new_copy.wait_recv()
            new_wide[...] = new[...].astype(F32)

        @pl.when(jnp.logical_and(t >= begin, t < begin + 3))
        def _():
            @pl.loop(0, per)
            def _(i):
                b = (t - begin) * per + i

                @pl.when(b < batches)
                def _():
                    attend(0, b)

        @pl.when(t == begin + 2)
        def _():
            spread_group(0, first_heads)

        @pl.when(jnp.logical_and(t >= LAG, t < chunks + LAG))
        def _():
            c = t - LAG
            slot = c % SLOTS
            wait_bytes(pair_in.at[c], pair_recv.at[c])
            for k, other in enumerate(others):
                line_out[c, k] = encode(mine[slot, other] + decode(pair_in[c, other], shift, 3), shift, 3)
                remote(
                    line_out.at[c, k], line_in.at[c, k], line_send, line_recv.at[c], {"wide": other * 2 + inner}
                ).start()
            kept[slot] = mine[slot, outer] + decode(pair_in[c, outer], shift, 3)

        @pl.when(jnp.logical_and(t >= 2 * LAG, t < chunks + 2 * LAG))
        def _():
            c = t - 2 * LAG
            wait_bytes(line_in.at[c], line_recv.at[c])
            summed = kept[c % SLOTS]
            for k in range(outers - 1):
                summed += decode(line_in[c, k], shift, 3)
            summed = summed.astype(BF16)

            @pl.when(c == 0)
            def _():
                new[half] = summed
                new_copy.start()

            @pl.when(c > 0)
            def _():
                h = c - 1
                query[h // GROUP, :, pl.ds(h % GROUP, 1), :] = summed.astype(F32)[:, None, :]

    early = 0
    if rest_heads:
        early = min(2, first_heads * dh // cols)

        @pl.loop(0, batches)
        def _(b):
            attend(1, b)
            for g in range(early):
                @pl.when(b == (g + 1) * batches // early - 1)
                def _():
                    forward(g)

        spread_group(first_heads, rest_heads)

    def piece_product(g, b):
        count = BLOCK // rows
        left = gathered[g, pl.ds(b * count, count)].reshape(BLOCK, cols)
        return jnp.dot(left, out_weights[g % AHEAD], preferred_element_type=F32)

    def arrive(g):
        wait_bytes(gathered.at[g, pl.ds(0, outers)], spread_pair.at[g])
        wait_bytes(out_weights.at[g % AHEAD], out_sem.at[g % AHEAD])

    total[...] = jnp.zeros_like(total)

    @pl.loop(0, pieces)
    def _(g):
        @pl.when(g >= early)
        def _():
            forward(g)

        @pl.when(g > 0)
        def _():
            arrive(g - 1)

            @pl.loop(0, 2 * blocks)
            def _(b):
                total[b] += piece_product(g - 1, b)

            @pl.when(g - 1 + AHEAD < pieces)
            def _():
                out_copy(g - 1 + AHEAD).start()

    last = pieces - 1
    arrive(last)

    @pl.loop(0, blocks)
    def _(b):
        at = (1 - half) * blocks + b
        half_out[b] = encode(total[at] + piece_product(last, at), 0, 2)
        remote(half_out.at[b], half_in.at[b], half_send, half_recv.at[b], across).start()

    @pl.loop(0, blocks)
    def _(b):
        at = half * blocks + b
        own = total[at] + piece_product(last, at)
        wait_bytes(half_in.at[b], half_recv.at[b])
        result[b] = (own + decode(half_in[b], 0, 2)).astype(BF16)

    pair_tokens.wait_send()
    new_copy.wait_send()
    wait_bytes(pair_out, pair_send)
    wait_bytes(line_out, line_send)
    wait_bytes(gathered.at[:, pl.ds(0, 2 * outers - 1)], spread_send)
    wait_bytes(half_out, half_send)


def shards(wide, tokens, w_query, w_keyval, cache_keys, cache_values, w_out):
    width = tokens.shape[1]
    total_rows = 2 * tokens.shape[0]
    rows, length, dh = cache_keys.shape
    outers = wide // 2
    features = w_query.shape[1]
    heads = features // dh
    chunks = heads + 1
    cols = 2 * dh
    pieces = features // cols
    groups = -(-heads // GROUP)
    blocks = total_rows // 2 // BLOCK
    vmem, dma = pltpu.VMEM, pltpu.SemaphoreType.DMA
    result = pl.pallas_call(
        functools.partial(block_kernel, wide),
        out_shape=jax.ShapeDtypeStruct((blocks, BLOCK, width), BF16),
        in_specs=[pl.BlockSpec(memory_space=pl.ANY)] * 6,
        out_specs=pl.BlockSpec(memory_space=vmem),
        scratch_shapes=[
            vmem((2, total_rows // 2, width), BF16),
            vmem((SLOTS, width, dh), BF16),
            vmem((wide, rows, dh), F32),
            vmem((SLOTS, outers, rows, dh), F32),
            vmem((SLOTS, rows, dh), F32),
            vmem((chunks, outers, rows, dh), BF16),
            vmem((chunks, outers, rows, dh), BF16),
            vmem((chunks, outers - 1, rows, dh), BF16),
            vmem((chunks, outers - 1, rows, dh), BF16),
            vmem((2, rows, dh), BF16),
            vmem((2, rows, dh), F32),
            vmem((groups, rows, GROUP, dh), F32),
            vmem((rows, GROUP, dh), F32),
            vmem((rows, length, dh), BF16),
            vmem((rows, length, dh), BF16),
            vmem((pieces, wide, rows, cols), BF16),
            vmem((AHEAD, cols, width), BF16),
            vmem((2 * blocks, BLOCK, width), F32),
            vmem((blocks, BLOCK, width), BF16),
            vmem((blocks, BLOCK, width), BF16),
            dma((SLOTS,)),
            dma((3,)),
            dma((2,)),
            dma,
            dma((chunks,)),
            dma,
            dma((chunks,)),
            dma((2,)),
            dma((AHEAD,)),
            dma,
            dma((pieces,)),
            dma((pieces,)),
            dma,
            dma((blocks,)),
        ],
        compiler_params=pltpu.CompilerParams(
            collective_id=0, has_side_effects=True, vmem_limit_bytes=62 * 2**20
        ),
        cost_estimate=pl.CostEstimate(
            flops=2 * total_rows * width * (chunks * dh + features),
            bytes_accessed=2 * width * (chunks * dh + features) + 4 * rows * length * dh,
            transcendentals=rows * heads * length,
        ),
    )(tokens, w_query, w_keyval, cache_keys, cache_values, w_out)
    return result.reshape(blocks * BLOCK, width)


def solution(mesh):
    in_specs = (
        P(("groups", "narrow"), "wide"),
        P("wide", "narrow"),
        P("wide", None),
        P(("groups", "wide"), None, None),
        P(("groups", "wide"), None, None),
        P("narrow", "wide"),
    )
    out_specs = P(("groups", "narrow"), "wide")
    return jax.shard_map(
        functools.partial(shards, mesh.shape["wide"]),
        mesh=mesh, in_specs=in_specs, out_specs=out_specs, check_vma=False,
    )
```

```python
import functools
import math

import jax
import jax.numpy as jnp
from jax import lax
from jax.experimental import pallas as pl
from jax.experimental.pallas import tpu as pltpu
from jax.sharding import PartitionSpec as P

MESH = pl.DeviceIdType.MESH
F32 = jnp.float32
BF16 = jnp.bfloat16
LAG = 3
SLOTS = LAG + 1
BLOCK = 128
GROUP = 8
BATCH = 8
AHEAD = 3


def bound_shift(width):
    return 15 - math.ceil(math.log2(2 * width * 6.0 * 0.09375))


def encode(x, shift, squarings):
    power = x * 2.0**shift
    for _ in range(squarings):
        power = power * power
    return jnp.where(x < 0, -power, power).astype(BF16)


def decode(y, shift, squarings):
    y = y.astype(F32)
    x = jnp.exp2(jnp.log2(jnp.abs(y)) * 0.5**squarings - shift)
    return jnp.where(y < 0, -x, x)


def wait_bytes(ref, sem):
    pltpu.make_async_copy(ref, ref, sem).wait()


def peers(wide):
    outers = wide // 2
    me = lax.axis_index("wide")
    outer, inner = me // 2, me % 2
    partner = outer * 2 + 1 - inner
    others = [lax.rem(outer + k, outers) for k in range(1, outers)]
    return outers, me, outer, inner, partner, others


def greet(wide):
    outers, _, _, inner, partner, others = peers(wide)
    barrier = pltpu.get_barrier_semaphore()
    pl.semaphore_signal(barrier, inc=1, device_id={"narrow": 1 - lax.axis_index("narrow")}, device_id_type=MESH)
    pl.semaphore_signal(barrier, inc=1, device_id={"wide": partner}, device_id_type=MESH)
    for other in others:
        pl.semaphore_signal(barrier, inc=1, device_id={"wide": other * 2 + inner}, device_id_type=MESH)
    pl.semaphore_wait(barrier, 1 + outers)


def remote(src, dst, send, recv, where):
    return pltpu.make_async_remote_copy(
        src_ref=src, dst_ref=dst, send_sem=send, recv_sem=recv, device_id=where, device_id_type=MESH
    )


def block_kernel(
    wide, tokens, w_query, w_keyval, cache_keys, cache_values, w_out, result,
    tok, weights, product, mine, kept, pair_out, pair_in, line_out, line_in, new, new_wide,
    query, mixed, keys, values, gathered, out_weights, total, half_out, half_in,
    w_sem, tok_sem, cache_sem, pair_send, pair_recv, line_send, line_recv, new_sem,
    out_sem, spread_send, hop_send, hop_recv, spread_pair, half_send, half_recv,
):
    outers, me, outer, inner, partner, others = peers(wide)
    half = lax.axis_index("narrow")
    across = {"narrow": 1 - half}
    chunks, _, rows, dh = pair_out.shape
    heads = chunks - 1
    width = tokens.shape[1]
    shift = bound_shift(width)
    scale = dh**-0.5
    pieces, cols = gathered.shape[0], gathered.shape[3]
    blocks = half_out.shape[0]
    batches = rows // BATCH
    first_heads = min(GROUP, heads)
    rest_heads = heads - first_heads
    begin = first_heads + 2 * LAG + 1
    per = -(-batches // 3)

    def weight_copy(c, slot):
        columns = pl.ds(pl.multiple_of((c - 1) * dh, dh), dh)
        return pltpu.make_async_copy(w_query.at[:, columns], weights.at[slot], w_sem.at[slot])

    def out_copy(g):
        take = pl.ds(pl.multiple_of(g * cols, cols), cols)
        slot = g % AHEAD
        return pltpu.make_async_copy(w_out.at[take, :], out_weights.at[slot], out_sem.at[slot])

    own_tokens = pltpu.make_async_copy(tokens, tok.at[half], tok_sem.at[0])
    own_tokens.start()
    columns = pl.ds(pl.multiple_of(half * dh, dh), dh)
    pltpu.make_async_copy(w_keyval.at[:, columns], weights.at[0], w_sem.at[0]).start()
    greet(wide)
    pair_tokens = remote(tokens, tok.at[half], tok_sem.at[1], tok_sem.at[2], across)
    pair_tokens.start()

    @pl.loop(1, SLOTS)
    def _(c):
        weight_copy(c, c).start()

    key_copy = pltpu.make_async_copy(cache_keys, keys, cache_sem.at[0])
    value_copy = pltpu.make_async_copy(cache_values, values, cache_sem.at[1])
    query[...] = jnp.zeros_like(query)
    own_tokens.wait()
    pair_tokens.wait_recv()

    new_copy = remote(new.at[half], new.at[half], new_sem.at[0], new_sem.at[1], across)

    def spread(g, block, where, recv):
        remote(
            gathered.at[g, block], gathered.at[g, block], spread_send, recv, {"wide": where}
        ).start()

    def may_send(k, up):
        if up:
            return jnp.logical_and(outer >= k, outer + 1 < outers)
        return jnp.logical_and(outer + k < outers, outer >= 1)

    def hop(g, k, up):
        block = (outer - k if up else outer + k) * 2 + inner
        where = (outer + 1 if up else outer - 1) * 2 + inner
        at = (g * (outers - 1) + k) * 2 + up
        piece = gathered.at[g, block]
        return remote(piece, piece, hop_send.at[at], hop_recv.at[at], {"wide": where})

    def forward(g, k):
        for up in (0, 1):
            source = outer - 1 - k if up else outer + 1 + k

            @pl.when(source >= 0 if up else source < outers)
            def _():
                at = (g * (outers - 1) + k) * 2 + up
                block = source * 2 + inner
                wait_bytes(gathered.at[g, block], hop_recv.at[at])
                if k + 1 < outers - 1:
                    @pl.when(may_send(k + 1, up))
                    def _():
                        hop(g, k + 1, up).start()
                spread(g, block, partner, spread_pair.at[g])

    def forward_step(t):
        for k in range(outers - 1):
            @pl.when(jnp.logical_and(t >= k, t - k < pieces))
            def _():
                forward(t - k, k)

    def attend(group, b):
        take = pl.ds(pl.multiple_of(b * BATCH, BATCH), BATCH)
        q = query[group, take]
        cached = lax.dot_general(
            q.astype(BF16), keys[take], (((2,), (2,)), ((0,), (0,))), preferred_element_type=F32
        ) * scale
        new_key = new_wide[0, take][:, None, :]
        new_value = new_wide[1, take][:, None, :]
        own = jnp.sum(q * new_key, axis=-1, keepdims=True) * scale
        top = jnp.maximum(jnp.max(cached, axis=-1, keepdims=True), own)
        cached_exp = jnp.exp(cached - top)
        own_exp = jnp.exp(own - top)
        denominator = jnp.sum(cached_exp, axis=-1, keepdims=True) + own_exp
        probs = (cached_exp / denominator).astype(BF16)
        probs_own = (own_exp / denominator).astype(BF16).astype(F32)
        out = lax.dot_general(
            probs, values[take], (((2,), (1,)), ((0,), (0,))), preferred_element_type=F32
        )
        mixed[take] = out + probs_own * new_value

    def spread_group(first, count):
        for j in range(count):
            piece, at = divmod((first + j) * dh, cols)
            gathered[piece, me, :, at : at + dh] = mixed[:, j, :].astype(BF16)
        for g in range(first * dh // cols, (first + count) * dh // cols):
            for up in (0, 1):
                @pl.when(may_send(0, up))
                def _():
                    hop(g, 0, up).start()
            spread(g, me, partner, spread_pair.at[g])

    @pl.loop(0, max(chunks + 2 * LAG, begin + 3))
    def _(t):
        @pl.when(t < chunks)
        def _():
            slot = t % SLOTS
            wait_bytes(weights.at[slot], w_sem.at[slot])
            product[...] = jnp.dot(
                tok[...].reshape(wide * rows, width), weights[slot], preferred_element_type=F32
            ).reshape(wide, rows, dh)
            for o in range(outers):
                pair_out[t, o] = encode(product[2 * o + 1 - inner], shift, 3)
                mine[slot, o] = product[2 * o + inner]
            remote(pair_out.at[t], pair_in.at[t], pair_send, pair_recv.at[t], {"wide": partner}).start()

            @pl.when(t + SLOTS < chunks)
            def _():
                weight_copy(t + SLOTS, slot).start()

        @pl.when(t == LAG)
        def _():
            key_copy.start()
            value_copy.start()

            @pl.loop(0, AHEAD)
            def _(g):
                out_copy(g).start()

        @pl.when(t == begin)
        def _():
            key_copy.wait()
            value_copy.wait()
            new_copy.wait_recv()
            new_wide[...] = new[...].astype(F32)

        @pl.when(jnp.logical_and(t >= begin, t < begin + 3))
        def _():
            @pl.loop(0, per)
            def _(i):
                b = (t - begin) * per + i

                @pl.when(b < batches)
                def _():
                    attend(0, b)

        @pl.when(t == begin + 2)
        def _():
            spread_group(0, first_heads)

        @pl.when(jnp.logical_and(t >= LAG, t < chunks + LAG))
        def _():
            c = t - LAG
            slot = c % SLOTS
            wait_bytes(pair_in.at[c], pair_recv.at[c])
            for k, other in enumerate(others):
                line_out[c, k] = encode(mine[slot, other] + decode(pair_in[c, other], shift, 3), shift, 3)
                remote(
                    line_out.at[c, k], line_in.at[c, k], line_send, line_recv.at[c], {"wide": other * 2 + inner}
                ).start()
            kept[slot] = mine[slot, outer] + decode(pair_in[c, outer], shift, 3)

        @pl.when(jnp.logical_and(t >= 2 * LAG, t < chunks + 2 * LAG))
        def _():
            c = t - 2 * LAG
            wait_bytes(line_in.at[c], line_recv.at[c])
            summed = kept[c % SLOTS]
            for k in range(outers - 1):
                summed += decode(line_in[c, k], shift, 3)
            summed = summed.astype(BF16)

            @pl.when(c == 0)
            def _():
                new[half] = summed
                new_copy.start()

            @pl.when(c > 0)
            def _():
                h = c - 1
                query[h // GROUP, :, pl.ds(h % GROUP, 1), :] = summed.astype(F32)[:, None, :]

    early = 0
    if rest_heads:
        early = min(2, first_heads * dh // cols)

        @pl.loop(0, batches)
        def _(b):
            attend(1, b)
            for g in range(early):
                @pl.when(b == (g + 1) * batches // early - 1)
                def _():
                    forward_step(g)

        spread_group(first_heads, rest_heads)

    def piece_product(g, b):
        count = BLOCK // rows
        left = gathered[g, pl.ds(b * count, count)].reshape(BLOCK, cols)
        return jnp.dot(left, out_weights[g % AHEAD], preferred_element_type=F32)

    def arrive(g):
        wait_bytes(gathered.at[g, pl.ds(0, outers)], spread_pair.at[g])
        wait_bytes(out_weights.at[g % AHEAD], out_sem.at[g % AHEAD])

    total[...] = jnp.zeros_like(total)

    @pl.loop(0, pieces + outers - 2)
    def _(t):
        @pl.when(t >= early)
        def _():
            forward_step(t)

        @pl.when(t >= outers - 1)
        def _():
            g = t - (outers - 1)
            arrive(g)

            @pl.loop(0, 2 * blocks)
            def _(b):
                total[b] += piece_product(g, b)

            @pl.when(g + AHEAD < pieces)
            def _():
                out_copy(g + AHEAD).start()

    last = pieces - 1
    arrive(last)

    @pl.loop(0, blocks)
    def _(b):
        at = (1 - half) * blocks + b
        half_out[b] = encode(total[at] + piece_product(last, at), 0, 2)
        remote(half_out.at[b], half_in.at[b], half_send, half_recv.at[b], across).start()

    @pl.loop(0, blocks)
    def _(b):
        at = half * blocks + b
        own = total[at] + piece_product(last, at)
        wait_bytes(half_in.at[b], half_recv.at[b])
        result[b] = (own + decode(half_in[b], 0, 2)).astype(BF16)

    pair_tokens.wait_send()
    new_copy.wait_send()
    wait_bytes(pair_out, pair_send)
    wait_bytes(line_out, line_send)
    wait_bytes(gathered.at[:, pl.ds(0, outers)], spread_send)

    @pl.loop(0, pieces)
    def _(g):
        for k in range(outers - 1):
            for up in (0, 1):
                @pl.when(may_send(k, up))
                def _():
                    wait_bytes(gathered.at[g, 0], hop_send.at[(g * (outers - 1) + k) * 2 + up])

    wait_bytes(half_out, half_send)


def shards(wide, tokens, w_query, w_keyval, cache_keys, cache_values, w_out):
    width = tokens.shape[1]
    total_rows = 2 * tokens.shape[0]
    rows, length, dh = cache_keys.shape
    outers = wide // 2
    features = w_query.shape[1]
    heads = features // dh
    chunks = heads + 1
    cols = 2 * dh
    pieces = features // cols
    groups = -(-heads // GROUP)
    blocks = total_rows // 2 // BLOCK
    vmem, dma = pltpu.VMEM, pltpu.SemaphoreType.DMA
    result = pl.pallas_call(
        functools.partial(block_kernel, wide),
        out_shape=jax.ShapeDtypeStruct((blocks, BLOCK, width), BF16),
        in_specs=[pl.BlockSpec(memory_space=pl.ANY)] * 6,
        out_specs=pl.BlockSpec(memory_space=vmem),
        scratch_shapes=[
            vmem((2, total_rows // 2, width), BF16),
            vmem((SLOTS, width, dh), BF16),
            vmem((wide, rows, dh), F32),
            vmem((SLOTS, outers, rows, dh), F32),
            vmem((SLOTS, rows, dh), F32),
            vmem((chunks, outers, rows, dh), BF16),
            vmem((chunks, outers, rows, dh), BF16),
            vmem((chunks, outers - 1, rows, dh), BF16),
            vmem((chunks, outers - 1, rows, dh), BF16),
            vmem((2, rows, dh), BF16),
            vmem((2, rows, dh), F32),
            vmem((groups, rows, GROUP, dh), F32),
            vmem((rows, GROUP, dh), F32),
            vmem((rows, length, dh), BF16),
            vmem((rows, length, dh), BF16),
            vmem((pieces, wide, rows, cols), BF16),
            vmem((AHEAD, cols, width), BF16),
            vmem((2 * blocks, BLOCK, width), F32),
            vmem((blocks, BLOCK, width), BF16),
            vmem((blocks, BLOCK, width), BF16),
            dma((SLOTS,)),
            dma((3,)),
            dma((2,)),
            dma,
            dma((chunks,)),
            dma,
            dma((chunks,)),
            dma((2,)),
            dma((AHEAD,)),
            dma,
            dma((pieces * (outers - 1) * 2,)),
            dma((pieces * (outers - 1) * 2,)),
            dma((pieces,)),
            dma,
            dma((blocks,)),
        ],
        compiler_params=pltpu.CompilerParams(
            collective_id=0, has_side_effects=True, vmem_limit_bytes=62 * 2**20
        ),
        cost_estimate=pl.CostEstimate(
            flops=2 * total_rows * width * (chunks * dh + features),
            bytes_accessed=2 * width * (chunks * dh + features) + 4 * rows * length * dh,
            transcendentals=rows * heads * length,
        ),
    )(tokens, w_query, w_keyval, cache_keys, cache_values, w_out)
    return result.reshape(blocks * BLOCK, width)


def solution(mesh):
    in_specs = (
        P(("groups", "narrow"), "wide"),
        P("wide", "narrow"),
        P("wide", None),
        P(("groups", "wide"), None, None),
        P(("groups", "wide"), None, None),
        P("narrow", "wide"),
    )
    out_specs = P(("groups", "narrow"), "wide")
    return jax.shard_map(
        functools.partial(shards, mesh.shape["wide"]),
        mesh=mesh, in_specs=in_specs, out_specs=out_specs, check_vma=False,
    )
```

```python
import functools
import math

import jax
import jax.numpy as jnp
from jax import lax
from jax.experimental import pallas as pl
from jax.experimental.pallas import tpu as pltpu
from jax.sharding import PartitionSpec as P

MESH = pl.DeviceIdType.MESH
F32 = jnp.float32
BF16 = jnp.bfloat16
LAG = 2
SLOTS = LAG + 1
BLOCK = 128
GROUP = 8
BATCH = 8
AHEAD = 3


def bound_shift(width):
    return 15 - math.ceil(math.log2(2 * width * 6.0 * 0.09375))


def encode(x, shift, squarings):
    power = x * 2.0**shift
    for _ in range(squarings):
        power = power * power
    return jnp.where(x < 0, -power, power).astype(BF16)


def decode(y, shift, squarings):
    y = y.astype(F32)
    x = jnp.exp2(jnp.log2(jnp.abs(y)) * 0.5**squarings - shift)
    return jnp.where(y < 0, -x, x)


def wait_bytes(ref, sem):
    pltpu.make_async_copy(ref, ref, sem).wait()


def peers(wide):
    outers = wide // 2
    me = lax.axis_index("wide")
    outer, inner = me // 2, me % 2
    partner = outer * 2 + 1 - inner
    others = [lax.rem(outer + k, outers) for k in range(1, outers)]
    return outers, me, outer, inner, partner, others


def greet(wide):
    outers, _, _, inner, partner, others = peers(wide)
    barrier = pltpu.get_barrier_semaphore()
    pl.semaphore_signal(barrier, inc=1, device_id={"narrow": 1 - lax.axis_index("narrow")}, device_id_type=MESH)
    pl.semaphore_signal(barrier, inc=1, device_id={"wide": partner}, device_id_type=MESH)
    for other in others:
        pl.semaphore_signal(barrier, inc=1, device_id={"wide": other * 2 + inner}, device_id_type=MESH)
    pl.semaphore_wait(barrier, 1 + outers)


def remote(src, dst, send, recv, where):
    return pltpu.make_async_remote_copy(
        src_ref=src, dst_ref=dst, send_sem=send, recv_sem=recv, device_id=where, device_id_type=MESH
    )


def block_kernel(
    wide, tokens, w_query, w_keyval, cache_keys, cache_values, w_out, result,
    tok, weights, product, mine, kept, pair_out, pair_in, line_out, line_in, new, new_wide,
    query, mixed, keys, values, gathered, out_weights, total, half_out, half_in,
    w_sem, tok_sem, cache_sem, pair_send, pair_recv, line_send, line_recv, new_sem,
    out_sem, spread_send, hop_send, hop_recv, spread_pair, half_send, half_recv,
):
    outers, me, outer, inner, partner, others = peers(wide)
    half = lax.axis_index("narrow")
    across = {"narrow": 1 - half}
    chunks, _, rows, dh = pair_out.shape
    heads = chunks - 1
    width = tokens.shape[1]
    shift = bound_shift(width)
    scale = dh**-0.5
    pieces, cols = gathered.shape[0], gathered.shape[3]
    blocks = half_out.shape[0]
    batches = rows // BATCH
    first_heads = min(GROUP, heads)
    rest_heads = heads - first_heads
    begin = first_heads + 2 * LAG + 1
    per = -(-batches // 3)

    def weight_copy(c, slot):
        columns = pl.ds(pl.multiple_of((c - 1) * dh, dh), dh)
        return pltpu.make_async_copy(w_query.at[:, columns], weights.at[slot], w_sem.at[slot])

    def out_copy(g):
        take = pl.ds(pl.multiple_of(g * cols, cols), cols)
        slot = g % AHEAD
        return pltpu.make_async_copy(w_out.at[take, :], out_weights.at[slot], out_sem.at[slot])

    own_tokens = pltpu.make_async_copy(tokens, tok.at[half], tok_sem.at[0])
    own_tokens.start()
    columns = pl.ds(pl.multiple_of(half * dh, dh), dh)
    pltpu.make_async_copy(w_keyval.at[:, columns], weights.at[0], w_sem.at[0]).start()
    greet(wide)
    pair_tokens = remote(tokens, tok.at[half], tok_sem.at[1], tok_sem.at[2], across)
    pair_tokens.start()

    @pl.loop(1, SLOTS)
    def _(c):
        weight_copy(c, c).start()

    key_copy = pltpu.make_async_copy(cache_keys, keys, cache_sem.at[0])
    value_copy = pltpu.make_async_copy(cache_values, values, cache_sem.at[1])
    query[...] = jnp.zeros_like(query)
    own_tokens.wait()
    pair_tokens.wait_recv()

    new_copy = remote(new.at[half], new.at[half], new_sem.at[0], new_sem.at[1], across)

    def spread(g, block, where, recv):
        remote(
            gathered.at[g, block], gathered.at[g, block], spread_send, recv, {"wide": where}
        ).start()

    def may_send(k, up):
        if up:
            return jnp.logical_and(outer >= k, outer + 1 < outers)
        return jnp.logical_and(outer + k < outers, outer >= 1)

    def hop(g, k, up):
        block = (outer - k if up else outer + k) * 2 + inner
        where = (outer + 1 if up else outer - 1) * 2 + inner
        at = (g * (outers - 1) + k) * 2 + up
        piece = gathered.at[g, block]
        return remote(piece, piece, hop_send.at[at], hop_recv.at[at], {"wide": where})

    def forward(g, k):
        for up in (0, 1):
            source = outer - 1 - k if up else outer + 1 + k

            @pl.when(source >= 0 if up else source < outers)
            def _():
                at = (g * (outers - 1) + k) * 2 + up
                block = source * 2 + inner
                wait_bytes(gathered.at[g, block], hop_recv.at[at])
                if k + 1 < outers - 1:
                    @pl.when(may_send(k + 1, up))
                    def _():
                        hop(g, k + 1, up).start()
                spread(g, block, partner, spread_pair.at[g])

    def forward_step(t):
        for k in range(outers - 1):
            @pl.when(jnp.logical_and(t >= k, t - k < pieces))
            def _():
                forward(t - k, k)

    def attend(group, b):
        take = pl.ds(pl.multiple_of(b * BATCH, BATCH), BATCH)
        q = query[group, take]
        cached = lax.dot_general(
            q.astype(BF16), keys[take], (((2,), (2,)), ((0,), (0,))), preferred_element_type=F32
        ) * scale
        new_key = new_wide[0, take][:, None, :]
        new_value = new_wide[1, take][:, None, :]
        own = jnp.sum(q * new_key, axis=-1, keepdims=True) * scale
        top = jnp.maximum(jnp.max(cached, axis=-1, keepdims=True), own)
        cached_exp = jnp.exp(cached - top)
        own_exp = jnp.exp(own - top)
        denominator = jnp.sum(cached_exp, axis=-1, keepdims=True) + own_exp
        probs = (cached_exp / denominator).astype(BF16)
        probs_own = (own_exp / denominator).astype(BF16).astype(F32)
        out = lax.dot_general(
            probs, values[take], (((2,), (1,)), ((0,), (0,))), preferred_element_type=F32
        )
        mixed[take] = out + probs_own * new_value

    def spread_group(first, count):
        for j in range(count):
            piece, at = divmod((first + j) * dh, cols)
            gathered[piece, me, :, at : at + dh] = mixed[:, j, :].astype(BF16)
        for g in range(first * dh // cols, (first + count) * dh // cols):
            for up in (0, 1):
                @pl.when(may_send(0, up))
                def _():
                    hop(g, 0, up).start()
            spread(g, me, partner, spread_pair.at[g])

    @pl.loop(0, max(chunks + 2 * LAG, begin + 3))
    def _(t):
        @pl.when(t < chunks)
        def _():
            slot = t % SLOTS
            wait_bytes(weights.at[slot], w_sem.at[slot])
            product[...] = jnp.dot(
                tok[...].reshape(wide * rows, width), weights[slot], preferred_element_type=F32
            ).reshape(wide, rows, dh)
            for o in range(outers):
                pair_out[t, o] = encode(product[2 * o + 1 - inner], shift, 3)
                mine[slot, o] = product[2 * o + inner]
            remote(pair_out.at[t], pair_in.at[t], pair_send, pair_recv.at[t], {"wide": partner}).start()

            @pl.when(t + SLOTS < chunks)
            def _():
                weight_copy(t + SLOTS, slot).start()

        @pl.when(t == LAG)
        def _():
            key_copy.start()
            value_copy.start()

            @pl.loop(0, AHEAD)
            def _(g):
                out_copy(g).start()

        @pl.when(t == begin)
        def _():
            key_copy.wait()
            value_copy.wait()
            new_copy.wait_recv()
            new_wide[...] = new[...].astype(F32)

        @pl.when(jnp.logical_and(t >= begin, t < begin + 3))
        def _():
            @pl.loop(0, per)
            def _(i):
                b = (t - begin) * per + i

                @pl.when(b < batches)
                def _():
                    attend(0, b)

        @pl.when(t == begin + 2)
        def _():
            spread_group(0, first_heads)

        @pl.when(jnp.logical_and(t >= LAG, t < chunks + LAG))
        def _():
            c = t - LAG
            slot = c % SLOTS
            wait_bytes(pair_in.at[c], pair_recv.at[c])
            for k, other in enumerate(others):
                line_out[c, k] = encode(mine[slot, other] + decode(pair_in[c, other], shift, 3), shift, 3)
                remote(
                    line_out.at[c, k], line_in.at[c, k], line_send, line_recv.at[c], {"wide": other * 2 + inner}
                ).start()
            kept[slot] = mine[slot, outer] + decode(pair_in[c, outer], shift, 3)

        @pl.when(jnp.logical_and(t >= 2 * LAG, t < chunks + 2 * LAG))
        def _():
            c = t - 2 * LAG
            wait_bytes(line_in.at[c], line_recv.at[c])
            summed = kept[c % SLOTS]
            for k in range(outers - 1):
                summed += decode(line_in[c, k], shift, 3)
            summed = summed.astype(BF16)

            @pl.when(c == 0)
            def _():
                new[half] = summed
                new_copy.start()

            @pl.when(c > 0)
            def _():
                h = c - 1
                query[h // GROUP, :, pl.ds(h % GROUP, 1), :] = summed.astype(F32)[:, None, :]

    early = 0
    if rest_heads:
        early = min(2, first_heads * dh // cols)

        @pl.loop(0, batches)
        def _(b):
            attend(1, b)
            for g in range(early):
                @pl.when(b == (g + 1) * batches // early - 1)
                def _():
                    forward_step(g)

        spread_group(first_heads, rest_heads)

    def piece_product(g, b):
        count = BLOCK // rows
        left = gathered[g, pl.ds(b * count, count)].reshape(BLOCK, cols)
        return jnp.dot(left, out_weights[g % AHEAD], preferred_element_type=F32)

    def arrive(g):
        wait_bytes(gathered.at[g, pl.ds(0, outers)], spread_pair.at[g])
        wait_bytes(out_weights.at[g % AHEAD], out_sem.at[g % AHEAD])

    total[...] = jnp.zeros_like(total)

    @pl.loop(0, pieces + outers - 2)
    def _(t):
        @pl.when(t >= early)
        def _():
            forward_step(t)

        @pl.when(t >= outers - 1)
        def _():
            g = t - (outers - 1)
            arrive(g)

            @pl.loop(0, 2 * blocks)
            def _(b):
                total[b] += piece_product(g, b)

            @pl.when(g + AHEAD < pieces)
            def _():
                out_copy(g + AHEAD).start()

    last = pieces - 1
    arrive(last)

    @pl.loop(0, blocks)
    def _(b):
        at = (1 - half) * blocks + b
        half_out[b] = encode(total[at] + piece_product(last, at), 0, 2)
        remote(half_out.at[b], half_in.at[b], half_send, half_recv.at[b], across).start()

    @pl.loop(0, blocks)
    def _(b):
        at = half * blocks + b
        own = total[at] + piece_product(last, at)
        wait_bytes(half_in.at[b], half_recv.at[b])
        result[b] = (own + decode(half_in[b], 0, 2)).astype(BF16)

    pair_tokens.wait_send()
    new_copy.wait_send()
    wait_bytes(pair_out, pair_send)
    wait_bytes(line_out, line_send)
    wait_bytes(gathered.at[:, pl.ds(0, outers)], spread_send)

    @pl.loop(0, pieces)
    def _(g):
        for k in range(outers - 1):
            for up in (0, 1):
                @pl.when(may_send(k, up))
                def _():
                    wait_bytes(gathered.at[g, 0], hop_send.at[(g * (outers - 1) + k) * 2 + up])

    wait_bytes(half_out, half_send)


def shards(wide, tokens, w_query, w_keyval, cache_keys, cache_values, w_out):
    width = tokens.shape[1]
    total_rows = 2 * tokens.shape[0]
    rows, length, dh = cache_keys.shape
    outers = wide // 2
    features = w_query.shape[1]
    heads = features // dh
    chunks = heads + 1
    cols = 2 * dh
    pieces = features // cols
    groups = -(-heads // GROUP)
    blocks = total_rows // 2 // BLOCK
    vmem, dma = pltpu.VMEM, pltpu.SemaphoreType.DMA
    result = pl.pallas_call(
        functools.partial(block_kernel, wide),
        out_shape=jax.ShapeDtypeStruct((blocks, BLOCK, width), BF16),
        in_specs=[pl.BlockSpec(memory_space=pl.ANY)] * 6,
        out_specs=pl.BlockSpec(memory_space=vmem),
        scratch_shapes=[
            vmem((2, total_rows // 2, width), BF16),
            vmem((SLOTS, width, dh), BF16),
            vmem((wide, rows, dh), F32),
            vmem((SLOTS, outers, rows, dh), F32),
            vmem((SLOTS, rows, dh), F32),
            vmem((chunks, outers, rows, dh), BF16),
            vmem((chunks, outers, rows, dh), BF16),
            vmem((chunks, outers - 1, rows, dh), BF16),
            vmem((chunks, outers - 1, rows, dh), BF16),
            vmem((2, rows, dh), BF16),
            vmem((2, rows, dh), F32),
            vmem((groups, rows, GROUP, dh), F32),
            vmem((rows, GROUP, dh), F32),
            vmem((rows, length, dh), BF16),
            vmem((rows, length, dh), BF16),
            vmem((pieces, wide, rows, cols), BF16),
            vmem((AHEAD, cols, width), BF16),
            vmem((2 * blocks, BLOCK, width), F32),
            vmem((blocks, BLOCK, width), BF16),
            vmem((blocks, BLOCK, width), BF16),
            dma((SLOTS,)),
            dma((3,)),
            dma((2,)),
            dma,
            dma((chunks,)),
            dma,
            dma((chunks,)),
            dma((2,)),
            dma((AHEAD,)),
            dma,
            dma((pieces * (outers - 1) * 2,)),
            dma((pieces * (outers - 1) * 2,)),
            dma((pieces,)),
            dma,
            dma((blocks,)),
        ],
        compiler_params=pltpu.CompilerParams(
            collective_id=0, has_side_effects=True, vmem_limit_bytes=56 * 2**20
        ),
        cost_estimate=pl.CostEstimate(
            flops=2 * total_rows * width * (chunks * dh + features),
            bytes_accessed=2 * width * (chunks * dh + features) + 4 * rows * length * dh,
            transcendentals=rows * heads * length,
        ),
    )(tokens, w_query, w_keyval, cache_keys, cache_values, w_out)
    return result.reshape(blocks * BLOCK, width)


def solution(mesh):
    in_specs = (
        P(("groups", "narrow"), "wide"),
        P("wide", "narrow"),
        P("wide", None),
        P(("groups", "wide"), None, None),
        P(("groups", "wide"), None, None),
        P("narrow", "wide"),
    )
    out_specs = P(("groups", "narrow"), "wide")
    return jax.shard_map(
        functools.partial(shards, mesh.shape["wide"]),
        mesh=mesh, in_specs=in_specs, out_specs=out_specs, check_vma=False,
    )
```
